256 devices in a mesh: group: 8 (over x, y_hi), member: 32 (over y_lo, z, core).
Axes of the slice: x: 4, y: 4 (y_hi: 2, y_lo: 2; y = y_hi * 2 + y_lo), z: 8, core: 2. Of those that a mesh axis runs over, the one named last changes fastest.
Arguments:
- picture_embedding_matrix: bfloat16 [65536, 1152], P(('group', 'member')), may hold values from -1 to 1
- caption_embedding_matrix: bfloat16 [65536, 1152], P(('group', 'member')), may hold values from -1 to 1
- learned_sharpness: float32 [1], replicated, may hold values from 5 to 20
- learned_offset_entry: float32 [1], replicated, may hold values from -4 to -2
Outputs:
- grad_images: float32 [65536, 1152], P(('group', 'member'))
- grad_texts: float32 [65536, 1152], P(('group', 'member'))
The draws below stay inside these ranges and needn't reach their ends.
All inputs are finite; a program needn't handle non-finite values.
Results may differ from the reference program's by a relative error of at most 0.002.
Values may be sent and summed in bfloat16 or wider, within the bound.
No kernel may reach another device: no remote copies, remote signals or barrier semaphores. Data moves between devices by JAX's collectives and lax.ppermute only.
A program may use at most 192 MiB of HBM per device.

```python
import math
import jax
import jax.numpy as jnp
from jax import lax

D = 1152
ROWS = 256
GROUP_ROWS = 8192
TOTAL = 65536
N_GROUP = 8
N_MEMBER = 32


def paired_rows(key):
    base_key = jax.random.fold_in(key, 7301)
    image_key, noise_key, ratio_key = jax.random.split(base_key, 3)
    spread = 1.0 / math.sqrt(D)
    picture_features = jnp.clip(spread * jax.random.normal(image_key, (TOTAL, D), jnp.float32), -5.0 * spread, 5.0 * spread)
    noise_rows = jnp.clip(spread * jax.random.normal(noise_key, (TOTAL, D), jnp.float32), -5.0 * spread, 5.0 * spread)
    pair_ratio = jax.random.uniform(ratio_key, (TOTAL, 1), jnp.float32, 0.15, 0.35)
    caption_features = pair_ratio * picture_features + jnp.sqrt(1.0 - pair_ratio * pair_ratio) * noise_rows
    caption_features = jnp.clip(caption_features, -1.0, 1.0)
    return (picture_features, caption_features)


def draw_picture_embedding_matrix(key, part):
    return paired_rows(key)[0].astype(jnp.bfloat16)


def draw_caption_embedding_matrix(key, part):
    return paired_rows(key)[1].astype(jnp.bfloat16)


def setup_inputs(seed: int = 0) -> dict:
    arg_keys = jax.random.split(jax.random.key(seed), 5)
    return {
        "picture_embedding_matrix": draw_picture_embedding_matrix(jax.random.fold_in(arg_keys[4], 71), 0),
        "caption_embedding_matrix": draw_caption_embedding_matrix(jax.random.fold_in(arg_keys[4], 71), 0),
        "learned_sharpness": jnp.clip(jnp.exp(jax.random.uniform(arg_keys[2], (1,), jnp.float32, math.log(5.0), math.log(20.0))), 5.0, 20.0),
        "learned_offset_entry": jnp.clip(jax.random.uniform(arg_keys[3], (1,), jnp.float32, -4.0, -2.0), -4.0, -2.0),
    }


def weighting_factors(similarity_scores, match_polarity, sharpness_multiplier):
    return (-sharpness_multiplier * match_polarity * jax.nn.sigmoid(-match_polarity * similarity_scores)).astype(jnp.bfloat16)


def reference(picture_embedding_matrix, caption_embedding_matrix, learned_sharpness, learned_offset_entry):
    sharpness_multiplier = learned_sharpness[0]
    offset_amount = learned_offset_entry[0]
    img_blocks = picture_embedding_matrix.reshape(N_GROUP, GROUP_ROWS, D)
    txt_blocks = caption_embedding_matrix.reshape(N_GROUP, GROUP_ROWS, D)
    txt_before = jnp.roll(txt_blocks, 1, axis=0)
    matching_polarity = jnp.eye(GROUP_ROWS, dtype=jnp.float32) * 2.0 - 1.0

    def one_group(block_groups):
        picture_features, caption_features, before = block_groups
        similarity_scores = sharpness_multiplier * jnp.dot(picture_features, caption_features.T, preferred_element_type=jnp.float32) + offset_amount
        score_multipliers = weighting_factors(similarity_scores, matching_polarity, sharpness_multiplier)
        grad_img = jnp.dot(score_multipliers, caption_features, preferred_element_type=jnp.float32)
        grad_txt = jnp.dot(score_multipliers.T, picture_features, preferred_element_type=jnp.float32)
        picture_participant = picture_features.reshape(N_MEMBER, ROWS, D).astype(jnp.float32)
        earlier_participant = before.reshape(N_MEMBER, ROWS, D).astype(jnp.float32)
        earlier_scores = sharpness_multiplier * jnp.einsum("eun,ean->eua", picture_participant, earlier_participant) + offset_amount
        earlier_multipliers = weighting_factors(earlier_scores, -1.0, sharpness_multiplier).astype(jnp.float32)
        grad_img = grad_img + jnp.einsum("mrs,msd->mrd", earlier_multipliers, earlier_participant).reshape(GROUP_ROWS, D)
        returned = jnp.einsum("mrs,mrd->msd", earlier_multipliers, picture_participant).reshape(GROUP_ROWS, D)
        return grad_img, grad_txt, returned

    grad_img, grad_txt, returned = lax.map(one_group, (img_blocks, txt_blocks, txt_before))
    grad_txt = grad_txt + jnp.roll(returned, -1, axis=0)
    return grad_img.reshape(TOTAL, D), grad_txt.reshape(TOTAL, D)
```

```python
import functools

import jax
import jax.numpy as jnp
from jax import lax
from jax.experimental import pallas as pl
from jax.experimental.pallas import tpu as pltpu
from jax.sharding import PartitionSpec as P

GROUPS, COLUMNS, RING, CORES = 8, 2, 8, 2
MEMBERS = COLUMNS * RING * CORES
RETURN_TYPE = jnp.bfloat16


def move(rows, group=0, column=0, ring=0, core=0):
    pairs = []
    by_core = group if isinstance(group, tuple) else (group, group)
    for g in range(GROUPS):
        for y in range(COLUMNS):
            for z in range(RING):
                for c in range(CORES):
                    here = ((g * COLUMNS + y) * RING + z) * CORES + c
                    there = (g + by_core[c]) % GROUPS
                    there = there * COLUMNS + (y + column) % COLUMNS
                    there = there * RING + (z + ring) % RING
                    there = there * CORES + (c + core) % CORES
                    pairs.append((here, there))
    return lax.ppermute(rows, ("group", "member"), pairs)


def after(rows, event):
    return lax.optimization_barrier((rows, event))[0]


def weights(scores, sharpness, offset, diagonal):
    logits = sharpness * scores + offset
    if not diagonal:
        return (sharpness / (1.0 + jnp.exp(-logits))).astype(jnp.bfloat16)
    rows = lax.broadcasted_iota(jnp.int32, logits.shape, 0)
    columns = lax.broadcasted_iota(jnp.int32, logits.shape, 1)
    polarity = jnp.where(rows == columns, 1.0, -1.0).astype(jnp.float32)
    return (-sharpness * polarity / (1.0 + jnp.exp(polarity * logits))).astype(jnp.bfloat16)


def terms_kernel(pairs, n_queries, n_keys, has_total, scalars, *refs):
    queries = refs[:n_queries]
    keys = refs[n_queries : n_queries + n_keys]
    totals = refs[n_queries + n_keys : len(refs) - n_queries] if has_total else ()
    outs = refs[len(refs) - n_queries :]
    sharpness, offset = scalars[0], scalars[1]
    for q in range(n_queries):
        total = totals[q][...] if has_total else None
        for k, diagonal in pairs[q]:
            scores = lax.dot_general(
                queries[q][...], keys[k][...], (((1,), (1,)), ((), ())), preferred_element_type=jnp.float32
            )
            part = jnp.dot(
                weights(scores, sharpness, offset, diagonal), keys[k][...], preferred_element_type=jnp.float32
            )
            total = part if total is None else total + part
        outs[q][...] = total.astype(outs[q].dtype)


def add_terms(scalars, queries, keys, totals=None, pairs=None, dtype=jnp.float32):
    if pairs is None:
        pairs = tuple(tuple((k, False) for k in range(len(keys))) for _ in queries)
    rows, width = queries[0].shape
    blocks = sum(len(p) for p in pairs)
    vmem = pl.BlockSpec(memory_space=pltpu.VMEM)
    arguments = (scalars, *queries, *keys, *(totals or ()))
    return pl.pallas_call(
        functools.partial(terms_kernel, pairs, len(queries), len(keys), totals is not None),
        out_shape=[jax.ShapeDtypeStruct((rows, width), dtype) for _ in queries],
        in_specs=[pl.BlockSpec(memory_space=pltpu.SMEM)] + [vmem] * (len(arguments) - 1),
        out_specs=[vmem] * len(queries),
        compiler_params=pltpu.CompilerParams(vmem_limit_bytes=16 * 1024 * 1024),
        cost_estimate=pl.CostEstimate(
            flops=4 * blocks * rows * rows * width,
            bytes_accessed=2 * rows * width * (len(queries) * 5 + len(keys)),
            transcendentals=blocks * rows * rows,
        ),
    )(*arguments)


def shards(images, texts, learned_sharpness, learned_offset_entry):
    scalars = jnp.concatenate([learned_sharpness, learned_offset_entry])
    first = lax.axis_index("member") % CORES == 0
    key = jnp.where(first, texts, images)
    query = jnp.where(first, images, texts)

    key_b = move(query, core=1)
    query_b = move(key, core=1)
    key_b, query_b = lax.optimization_barrier((key_b, query_b))

    beside = {
        1: lambda event: move(query, column=1),
        2: lambda event: move(after(key, event), column=1, core=1),
        3: lambda event: move(after(key, event), group=(1, -1)),
        4: lambda event: move(after(query, event), group=(-1, 1), core=1),
    }
    sent = {}
    right, left = {}, {}
    right["a", 0] = left["a", 0] = key
    right["b", 0] = left["b", 0] = key_b
    for step in range(1, 5):
        sent[step] = beside[step](right["a", step - 1])
        for half in "ab":
            if step < 4 or half == "a":
                right[half, step] = move(right[half, step - 1], ring=1)
            if step < 4 or half == "b":
                left[half, step] = move(left[half, step - 1], ring=-1)
            if step < 4:
                right[half, step], left[half, step] = lax.optimization_barrier(
                    (right[half, step], left[half, step])
                )
            if step < 4 and half == "a":
                right[half, step], sent[step] = lax.optimization_barrier((right[half, step], sent[step]))
    queries, lent, near = (query, query_b), (sent[1], sent[2]), (sent[3], sent[4])

    both = (*queries, *lent)
    totals = add_terms(
        scalars,
        both,
        (key, key_b),
        pairs=(
            ((0, True), (1, False)),
            ((0, False), (1, True)),
            ((0, False), (1, False)),
            ((0, False), (1, False)),
        ),
    )
    for step in range(1, 4):
        arrived = (right["a", step], left["a", step], right["b", step], left["b", step])
        pairs = [tuple((k, False) for k in range(4))] * 4
        if step == 3:
            arrived += near
            pairs[0] += ((4, False),)
            pairs[1] += ((5, False),)
        totals = add_terms(scalars, both, arrived, totals, tuple(pairs))
    arrived = (right["a", 4], left["b", 4])
    partner = add_terms(scalars, lent, arrived, totals[2:], dtype=RETURN_TYPE)
    back = move(partner[0], column=1), move(partner[1], column=1, core=1)
    own_b = add_terms(scalars, queries[1:], arrived, after(totals[1:2], partner))
    other = move(own_b[0], core=1)
    own = add_terms(scalars, queries[:1], arrived, after(totals[:1], own_b))

    mine = own[0] + back[0].astype(jnp.float32)
    other = other + back[1].astype(jnp.float32)
    return jnp.where(first, mine, other), jnp.where(first, other, mine)


def solution(mesh):
    rows = P(("group", "member"), None)
    return jax.shard_map(
        shards, mesh=mesh, in_specs=(rows, rows, P(), P()), out_specs=(rows, rows), check_vma=False
    )
```

```python
import functools

import jax
import jax.numpy as jnp
from jax import lax
from jax.experimental import pallas as pl
from jax.experimental.pallas import tpu as pltpu
from jax.sharding import PartitionSpec as P

GROUPS, COLUMNS, RING, CORES = 8, 2, 8, 2
MEMBERS = COLUMNS * RING * CORES
RETURN_TYPE = jnp.bfloat16


def move(rows, group=0, column=0, ring=0, core=0):
    pairs = []
    by_core = group if isinstance(group, tuple) else (group, group)
    for g in range(GROUPS):
        for y in range(COLUMNS):
            for z in range(RING):
                for c in range(CORES):
                    here = ((g * COLUMNS + y) * RING + z) * CORES + c
                    there = (g + by_core[c]) % GROUPS
                    there = there * COLUMNS + (y + column) % COLUMNS
                    there = there * RING + (z + ring) % RING
                    there = there * CORES + (c + core) % CORES
                    pairs.append((here, there))
    return lax.ppermute(rows, ("group", "member"), pairs)


def after(rows, event):
    return lax.optimization_barrier((rows, event))[0]


def wait(arriving, totals):
    return lax.optimization_barrier((arriving, totals))


def weights(scores, sharpness, offset, diagonal):
    logits = sharpness * scores + offset
    if not diagonal:
        return (sharpness / (1.0 + jnp.exp(-logits))).astype(jnp.bfloat16)
    rows = lax.broadcasted_iota(jnp.int32, logits.shape, 0)
    columns = lax.broadcasted_iota(jnp.int32, logits.shape, 1)
    polarity = jnp.where(rows == columns, 1.0, -1.0).astype(jnp.float32)
    return (-sharpness * polarity / (1.0 + jnp.exp(polarity * logits))).astype(jnp.bfloat16)


def terms_kernel(pairs, n_queries, n_keys, has_total, scalars, *refs):
    queries = refs[:n_queries]
    keys = refs[n_queries : n_queries + n_keys]
    totals = refs[n_queries + n_keys : len(refs) - n_queries] if has_total else ()
    outs = refs[len(refs) - n_queries :]
    sharpness, offset = scalars[0], scalars[1]
    for q in range(n_queries):
        total = totals[q][...] if has_total else None
        for k, diagonal in pairs[q]:
            scores = lax.dot_general(
                queries[q][...], keys[k][...], (((1,), (1,)), ((), ())), preferred_element_type=jnp.float32
            )
            part = jnp.dot(
                weights(scores, sharpness, offset, diagonal), keys[k][...], preferred_element_type=jnp.float32
            )
            total = part if total is None else total + part
        outs[q][...] = total.astype(outs[q].dtype)


def add_terms(scalars, queries, keys, totals=None, pairs=None, dtype=jnp.float32):
    if pairs is None:
        pairs = tuple(tuple((k, False) for k in range(len(keys))) for _ in queries)
    rows, width = queries[0].shape
    blocks = sum(len(p) for p in pairs)
    vmem = pl.BlockSpec(memory_space=pltpu.VMEM)
    arguments = (scalars, *queries, *keys, *(totals or ()))
    return pl.pallas_call(
        functools.partial(terms_kernel, pairs, len(queries), len(keys), totals is not None),
        out_shape=[jax.ShapeDtypeStruct((rows, width), dtype) for _ in queries],
        in_specs=[pl.BlockSpec(memory_space=pltpu.SMEM)] + [vmem] * (len(arguments) - 1),
        out_specs=[vmem] * len(queries),
        compiler_params=pltpu.CompilerParams(vmem_limit_bytes=16 * 1024 * 1024),
        cost_estimate=pl.CostEstimate(
            flops=4 * blocks * rows * rows * width,
            bytes_accessed=2 * rows * width * (len(queries) * 5 + len(keys)),
            transcendentals=blocks * rows * rows,
        ),
    )(*arguments)


def shards(images, texts, learned_sharpness, learned_offset_entry):
    scalars = jnp.concatenate([learned_sharpness, learned_offset_entry])
    first = lax.axis_index("member") % CORES == 0
    key = jnp.where(first, texts, images)
    query = jnp.where(first, images, texts)

    key_b = move(query, core=1)
    query_b = move(key, core=1)

    terms = functools.partial(add_terms, scalars)
    own, lent = (query, query_b), ()
    lent_a = move(query, column=1)
    a = move(key, ring=1), move(key, ring=-1)
    b = move(key_b, ring=1), move(key_b, ring=-1)
    total = terms(own, (key, key_b), pairs=(((0, True), (1, False)), ((0, False), (1, True))))

    (*a1, lent_a, _), total = wait((*a, lent_a, query_b), total)
    lent_b = move(after(key, a1), column=1, core=1)
    a = move(a1[0], ring=1), move(a1[1], ring=-1)
    total = terms(own, a1, total)

    b1, total = wait(b, total)
    b = move(b1[0], ring=1), move(b1[1], ring=-1)
    total = terms(own, b1, total)

    (*a2, lent_b), total = wait((*a, lent_b), total)
    near_a = move(after(key, a2), group=(1, -1))
    a = move(a2[0], ring=1), move(a2[1], ring=-1)
    lent = (lent_a, lent_b)
    loan = terms(lent, (key, key_b, *a1, *b1))

    b2, loan = wait(b, loan)
    b = move(b2[0], ring=1), move(b2[1], ring=-1)
    *total, loan_a, loan_b = terms((*own, *lent), a2, (*total, *loan))
    loan = loan_a, loan_b

    (*a3, near_a), loan = wait((*a, near_a), loan)
    near_b = move(after(query, a3), group=(-1, 1), core=1)
    a4 = move(a3[0], ring=1)
    *total, loan_a, loan_b = terms((*own, *lent), b2, (*total, *loan))
    loan = loan_a, loan_b

    b3, loan = wait(b, loan)
    b4 = move(b3[1], ring=-1)
    loan = terms(lent, (*a3, *b3), loan)
    total = after(total, loan)
    total = terms(
        own,
        (*a3, *b3, near_a, near_b),
        total,
        tuple(tuple((k, False) for k in (0, 1, 2, 3, 4 + q)) for q in range(2)),
    )

    last, total, loan = lax.optimization_barrier(((a4, b4), total, loan))
    loan_a = terms(lent[:1], last, loan[:1], dtype=RETURN_TYPE)
    back_a = move(loan_a[0], column=1)
    own_b = terms(own[1:], last, after(total[1:], loan_a))
    other = move(own_b[0], core=1)
    loan_b = terms(lent[1:], last, after(loan[1:], own_b), dtype=RETURN_TYPE)
    back_b = move(loan_b[0], column=1, core=1)
    own_a = terms(own[:1], last, after(total[:1], (loan_b, back_a)))

    mine = own_a[0] + back_a.astype(jnp.float32)
    other = other + back_b.astype(jnp.float32)
    return jnp.where(first, mine, other), jnp.where(first, other, mine)


def solution(mesh):
    rows = P(("group", "member"), None)
    return jax.shard_map(
        shards, mesh=mesh, in_specs=(rows, rows, P(), P()), out_specs=(rows, rows), check_vma=False
    )
```

```python
import functools

import jax
import jax.numpy as jnp
from jax import lax
from jax.experimental import pallas as pl
from jax.experimental.pallas import tpu as pltpu
from jax.sharding import PartitionSpec as P

GROUPS, COLUMNS, RING, CORES = 8, 2, 8, 2
MEMBERS = COLUMNS * RING * CORES
RETURN_TYPE = jnp.bfloat16


def move(rows, group=0, column=0, ring=0, core=0):
    pairs = []
    by_core = group if isinstance(group, tuple) else (group, group)
    for g in range(GROUPS):
        for y in range(COLUMNS):
            for z in range(RING):
                for c in range(CORES):
                    here = ((g * COLUMNS + y) * RING + z) * CORES + c
                    there = (g + by_core[c]) % GROUPS
                    there = there * COLUMNS + (y + column) % COLUMNS
                    there = there * RING + (z + ring) % RING
                    there = there * CORES + (c + core) % CORES
                    pairs.append((here, there))
    return lax.ppermute(rows, ("group", "member"), pairs)


def after(rows, event):
    return lax.optimization_barrier((rows, event))[0]


def wait(arriving, totals):
    return lax.optimization_barrier((arriving, totals))


def weights(scores, sharpness, offset, diagonal):
    logits = sharpness * scores + offset
    if not diagonal:
        return (sharpness / (1.0 + jnp.exp(-logits))).astype(jnp.bfloat16)
    rows = lax.broadcasted_iota(jnp.int32, logits.shape, 0)
    columns = lax.broadcasted_iota(jnp.int32, logits.shape, 1)
    polarity = jnp.where(rows == columns, 1.0, -1.0).astype(jnp.float32)
    return (-sharpness * polarity / (1.0 + jnp.exp(polarity * logits))).astype(jnp.bfloat16)


def terms_kernel(pairs, n_queries, n_keys, has_total, scalars, *refs):
    queries = refs[:n_queries]
    keys = refs[n_queries : n_queries + n_keys]
    totals = refs[n_queries + n_keys : len(refs) - n_queries] if has_total else ()
    outs = refs[len(refs) - n_queries :]
    sharpness, offset = scalars[0], scalars[1]
    blocks = [(q, k, diagonal) for q in range(n_queries) for k, diagonal in pairs[q]]

    def scores(q, k):
        contract = (((1,), (1,)), ((), ()))
        return lax.dot_general(queries[q][...], keys[k][...], contract, preferred_element_type=jnp.float32)

    total, ahead = None, scores(*blocks[0][:2])
    for n, (q, k, diagonal) in enumerate(blocks):
        now, ahead = ahead, scores(*blocks[n + 1][:2]) if n + 1 < len(blocks) else None
        part = jnp.dot(
            weights(now, sharpness, offset, diagonal), keys[k][...], preferred_element_type=jnp.float32
        )
        if n == 0 or blocks[n - 1][0] != q:
            total = totals[q][...] + part if has_total else part
        elif outs[q].dtype == jnp.float32:
            total = outs[q][...] + part
        else:
            total = total + part
        last = n + 1 == len(blocks) or blocks[n + 1][0] != q
        if last or outs[q].dtype == jnp.float32:
            outs[q][...] = total.astype(outs[q].dtype)


def add_terms(scalars, queries, keys, totals=None, pairs=None, dtype=jnp.float32):
    if pairs is None:
        pairs = tuple(tuple((k, False) for k in range(len(keys))) for _ in queries)
    rows, width = queries[0].shape
    blocks = sum(len(p) for p in pairs)
    vmem = pl.BlockSpec(memory_space=pltpu.VMEM)
    arguments = (scalars, *queries, *keys, *(totals or ()))
    return pl.pallas_call(
        functools.partial(terms_kernel, pairs, len(queries), len(keys), totals is not None),
        out_shape=[jax.ShapeDtypeStruct((rows, width), dtype) for _ in queries],
        in_specs=[pl.BlockSpec(memory_space=pltpu.SMEM)] + [vmem] * (len(arguments) - 1),
        out_specs=[vmem] * len(queries),
        compiler_params=pltpu.CompilerParams(vmem_limit_bytes=16 * 1024 * 1024),
        cost_estimate=pl.CostEstimate(
            flops=4 * blocks * rows * rows * width,
            bytes_accessed=2 * rows * width * (len(queries) * 5 + len(keys)),
            transcendentals=blocks * rows * rows,
        ),
    )(*arguments)


def shards(images, texts, learned_sharpness, learned_offset_entry):
    scalars = jnp.concatenate([learned_sharpness, learned_offset_entry])
    first = lax.axis_index("member") % CORES == 0
    key = jnp.where(first, texts, images)
    query = jnp.where(first, images, texts)

    key_b = move(query, core=1)
    query_b = move(key, core=1)

    terms = functools.partial(add_terms, scalars)
    own, lent = (query, query_b), ()
    lent_a = move(query, column=1)
    a = move(key, ring=1), move(key, ring=-1)
    b = move(key_b, ring=1), move(key_b, ring=-1)
    total = terms(own, (key, key_b), pairs=(((0, True), (1, False)), ((0, False), (1, True))))

    (*a1, lent_a, _), total = wait((*a, lent_a, query_b), total)
    lent_b = move(after(key, a1), column=1, core=1)
    a = move(a1[0], ring=1), move(a1[1], ring=-1)
    total = terms(own, a1, total)

    b1, total = wait(b, total)
    b = move(b1[0], ring=1), move(b1[1], ring=-1)
    total = terms(own, b1, total)

    (*a2, lent_b), total = wait((*a, lent_b), total)
    near_a = move(after(key, a2), group=(1, -1))
    a = move(a2[0], ring=1), move(a2[1], ring=-1)
    lent = (lent_a, lent_b)
    loan = terms(lent, (key, key_b, *a1, *b1))

    b2, loan = wait(b, loan)
    b = move(b2[0], ring=1), move(b2[1], ring=-1)
    *total, loan_a, loan_b = terms((*own, *lent), a2, (*total, *loan))
    loan = loan_a, loan_b

    (*a3, near_a), loan = wait((*a, near_a), loan)
    near_b = move(after(query, a3), group=(-1, 1), core=1)
    a4 = move(a3[0], ring=1)
    *total, loan_a, loan_b = terms((*own, *lent), b2, (*total, *loan))
    loan = loan_a, loan_b

    b3, loan = wait(b, loan)
    b4 = move(b3[1], ring=-1)
    loan = terms(lent, (*a3, *b3), loan)
    total = after(total, loan)
    total = terms(
        own,
        (*a3, *b3, near_a, near_b),
        total,
        tuple(tuple((k, False) for k in (0, 1, 2, 3, 4 + q)) for q in range(2)),
    )

    last, total, loan = lax.optimization_barrier(((a4, b4), total, loan))
    loan_a = terms(lent[:1], last, loan[:1], dtype=RETURN_TYPE)
    back_a = move(loan_a[0], column=1)
    own_b = terms(own[1:], last, after(total[1:], loan_a))
    other = move(own_b[0], core=1)
    loan_b = terms(lent[1:], last, after(loan[1:], own_b), dtype=RETURN_TYPE)
    back_b = move(loan_b[0], column=1, core=1)
    own_a = terms(own[:1], last, after(total[:1], (loan_b, back_a)))

    mine = own_a[0] + back_a.astype(jnp.float32)
    other = other + back_b.astype(jnp.float32)
    return jnp.where(first, mine, other), jnp.where(first, other, mine)


def solution(mesh):
    rows = P(("group", "member"), None)
    return jax.shard_map(
        shards, mesh=mesh, in_specs=(rows, rows, P(), P()), out_specs=(rows, rows), check_vma=False
    )
```

```python
import functools

import jax
import jax.numpy as jnp
from jax import lax
from jax.experimental import pallas as pl
from jax.experimental.pallas import tpu as pltpu
from jax.sharding import PartitionSpec as P

GROUPS, COLUMNS, RING, CORES = 8, 2, 8, 2
MEMBERS = COLUMNS * RING * CORES
RETURN_TYPE = jnp.bfloat16
THIRDS = slice(0, 96), slice(96, 192), slice(192, 256)


def move(rows, group=0, column=0, ring=0, core=0):
    pairs = []
    by_core = group if isinstance(group, tuple) else (group, group)
    for g in range(GROUPS):
        for y in range(COLUMNS):
            for z in range(RING):
                for c in range(CORES):
                    here = ((g * COLUMNS + y) * RING + z) * CORES + c
                    there = (g + by_core[c]) % GROUPS
                    there = there * COLUMNS + (y + column) % COLUMNS
                    there = there * RING + (z + ring) % RING
                    there = there * CORES + (c + core) % CORES
                    pairs.append((here, there))
    return lax.ppermute(rows, ("group", "member"), pairs)


def after(rows, event):
    return lax.optimization_barrier((rows, event))[0]


def wait(arriving, totals):
    return lax.optimization_barrier((arriving, totals))


def weights(scores, sharpness, offset, diagonal):
    logits = sharpness * scores + offset
    if not diagonal:
        return (sharpness / (1.0 + jnp.exp(-logits))).astype(jnp.bfloat16)
    rows = lax.broadcasted_iota(jnp.int32, logits.shape, 0)
    columns = lax.broadcasted_iota(jnp.int32, logits.shape, 1)
    polarity = jnp.where(rows == columns, 1.0, -1.0).astype(jnp.float32)
    return (-sharpness * polarity / (1.0 + jnp.exp(polarity * logits))).astype(jnp.bfloat16)


def terms_kernel(pairs, n_queries, n_keys, has_total, scalars, *refs):
    queries = refs[:n_queries]
    keys = refs[n_queries : n_queries + n_keys]
    totals = refs[n_queries + n_keys : len(refs) - n_queries] if has_total else ()
    outs = refs[len(refs) - n_queries :]
    sharpness, offset = scalars[0], scalars[1]
    blocks = [(q, k, diagonal) for q in range(n_queries) for k, diagonal in pairs[q]]

    def scores(q, k):
        contract = (((1,), (1,)), ((), ()))
        return lax.dot_general(queries[q][...], keys[k][...], contract, preferred_element_type=jnp.float32)

    total, ahead = None, scores(*blocks[0][:2])
    for n, (q, k, diagonal) in enumerate(blocks):
        now, ahead = ahead, scores(*blocks[n + 1][:2]) if n + 1 < len(blocks) else None
        part = jnp.dot(
            weights(now, sharpness, offset, diagonal), keys[k][...], preferred_element_type=jnp.float32
        )
        if n == 0 or blocks[n - 1][0] != q:
            total = totals[q][...] + part if has_total else part
        elif outs[q].dtype == jnp.float32:
            total = outs[q][...] + part
        else:
            total = total + part
        last = n + 1 == len(blocks) or blocks[n + 1][0] != q
        if last or outs[q].dtype == jnp.float32:
            outs[q][...] = total.astype(outs[q].dtype)


def add_terms(scalars, queries, keys, totals=None, pairs=None, dtype=jnp.float32):
    if pairs is None:
        pairs = tuple(tuple((k, False) for k in range(len(keys))) for _ in queries)
    rows, width = queries[0].shape
    blocks = sum(len(p) for p in pairs)
    vmem = pl.BlockSpec(memory_space=pltpu.VMEM)
    arguments = (scalars, *queries, *keys, *(totals or ()))
    return pl.pallas_call(
        functools.partial(terms_kernel, pairs, len(queries), len(keys), totals is not None),
        out_shape=[jax.ShapeDtypeStruct((rows, width), dtype) for _ in queries],
        in_specs=[pl.BlockSpec(memory_space=pltpu.SMEM)] + [vmem] * (len(arguments) - 1),
        out_specs=[vmem] * len(queries),
        compiler_params=pltpu.CompilerParams(vmem_limit_bytes=16 * 1024 * 1024),
        cost_estimate=pl.CostEstimate(
            flops=4 * blocks * rows * rows * width,
            bytes_accessed=2 * rows * width * (len(queries) * 5 + len(keys)),
            transcendentals=blocks * rows * rows,
        ),
    )(*arguments)


def shards(images, texts, learned_sharpness, learned_offset_entry):
    scalars = jnp.concatenate([learned_sharpness, learned_offset_entry])
    first = lax.axis_index("member") % CORES == 0
    key = jnp.where(first, texts, images)
    query = jnp.where(first, images, texts)

    key_b = move(query, core=1)
    query_b = move(key, core=1)

    terms = functools.partial(add_terms, scalars)
    own, lent = (query, query_b), ()
    lent_a = move(query, column=1)
    a = move(key, ring=1), move(key, ring=-1)
    b = move(key_b, ring=1), move(key_b, ring=-1)
    total = terms(own, (key, key_b), pairs=(((0, True), (1, False)), ((0, False), (1, True))))

    (*a1, lent_a, _), total = wait((*a, lent_a, query_b), total)
    lent_b = move(after(key, a1), column=1, core=1)
    a = move(a1[0], ring=1), move(a1[1], ring=-1)
    total = terms(own, a1, total)

    b1, total = wait(b, total)
    b = move(b1[0], ring=1), move(b1[1], ring=-1)
    total = terms(own, b1, total)

    (*a2, lent_b), total = wait((*a, lent_b), total)
    near_a = move(after(key, a2), group=(1, -1))
    a = move(a2[0], ring=1), move(a2[1], ring=-1)
    lent = (lent_a, lent_b)
    loan = terms(lent, (key, key_b, *a1, *b1))

    b2, loan = wait(b, loan)
    b = move(b2[0], ring=1), move(b2[1], ring=-1)
    *total, loan_a, loan_b = terms((*own, *lent), a2, (*total, *loan))
    loan = loan_a, loan_b

    (*a3, near_a), loan = wait((*a, near_a), loan)
    near_b = move(after(query, a3), group=(-1, 1), core=1)
    a4 = move(a3[0], ring=1)
    *total, loan_a, loan_b = terms((*own, *lent), b2, (*total, *loan))
    loan = loan_a, loan_b

    b3, loan = wait(b, loan)
    b4 = move(b3[1], ring=-1)
    loan = terms(lent, (*a3, *b3), loan)
    total = after(total, loan)
    total = terms(
        own,
        (*a3, *b3, near_a, near_b),
        total,
        tuple(tuple((k, False) for k in (0, 1, 2, 3, 4 + q)) for q in range(2)),
    )

    last, total, loan = lax.optimization_barrier(((a4, b4), total, loan))
    loan_a = terms(lent[:1], last, loan[:1], dtype=RETURN_TYPE)
    back_a = move(loan_a[0], column=1)
    loan_b = terms(lent[1:], last, after(loan[1:], loan_a), dtype=RETURN_TYPE)
    back_b = move(loan_b[0], column=1, core=1)
    own_b = terms(own[1:], last, after(total[1:], loan_b))
    other = jnp.concatenate([move(own_b[0][rows], core=1) for rows in THIRDS], axis=0)
    own_a = terms(own[:1], last, after(total[:1], own_b))

    mine = own_a[0] + back_a.astype(jnp.float32)
    other = other + back_b.astype(jnp.float32)
    return jnp.where(first, mine, other), jnp.where(first, other, mine)


def solution(mesh):
    rows = P(("group", "member"), None)
    return jax.shard_map(
        shards, mesh=mesh, in_specs=(rows, rows, P(), P()), out_specs=(rows, rows), check_vma=False
    )
```

```python
import functools

import jax
import jax.numpy as jnp
from jax import lax
from jax.experimental import pallas as pl
from jax.experimental.pallas import tpu as pltpu
from jax.sharding import PartitionSpec as P

GROUPS, COLUMNS, RING, CORES = 8, 2, 8, 2
MEMBERS = COLUMNS * RING * CORES
RETURN_TYPE = jnp.bfloat16
THIRDS = slice(0, 96), slice(96, 192), slice(192, 256)


def move(rows, group=0, column=0, ring=0, core=0):
    pairs = []
    by_core = group if isinstance(group, tuple) else (group, group)
    for g in range(GROUPS):
        for y in range(COLUMNS):
            for z in range(RING):
                for c in range(CORES):
                    here = ((g * COLUMNS + y) * RING + z) * CORES + c
                    there = (g + by_core[c]) % GROUPS
                    there = there * COLUMNS + (y + column) % COLUMNS
                    there = there * RING + (z + ring) % RING
                    there = there * CORES + (c + core) % CORES
                    pairs.append((here, there))
    return lax.ppermute(rows, ("group", "member"), pairs)


def after(rows, event):
    return lax.optimization_barrier((rows, event))[0]


def wait(arriving, totals):
    return lax.optimization_barrier((arriving, totals))


def weights(scores, sharpness, offset, diagonal):
    logits = sharpness * scores + offset
    if not diagonal:
        return (sharpness / (1.0 + jnp.exp(-logits))).astype(jnp.bfloat16)
    rows = lax.broadcasted_iota(jnp.int32, logits.shape, 0)
    columns = lax.broadcasted_iota(jnp.int32, logits.shape, 1)
    polarity = jnp.where(rows == columns, 1.0, -1.0).astype(jnp.float32)
    return (-sharpness * polarity / (1.0 + jnp.exp(polarity * logits))).astype(jnp.bfloat16)


def terms_kernel(pairs, n_queries, n_keys, has_total, scalars, *refs):
    queries = refs[:n_queries]
    keys = refs[n_queries : n_queries + n_keys]
    totals = refs[n_queries + n_keys : len(refs) - n_queries] if has_total else ()
    outs = refs[len(refs) - n_queries :]
    sharpness, offset = scalars[0], scalars[1]
    blocks = [(q, k, diagonal) for q in range(n_queries) for k, diagonal in pairs[q]]

    def scores(q, k):
        contract = (((1,), (1,)), ((), ()))
        return lax.dot_general(queries[q][...], keys[k][...], contract, preferred_element_type=jnp.float32)

    total, ahead = None, scores(*blocks[0][:2])
    for n, (q, k, diagonal) in enumerate(blocks):
        now, ahead = ahead, scores(*blocks[n + 1][:2]) if n + 1 < len(blocks) else None
        part = jnp.dot(
            weights(now, sharpness, offset, diagonal), keys[k][...], preferred_element_type=jnp.float32
        )
        if n == 0 or blocks[n - 1][0] != q:
            total = totals[q][...] + part if has_total else part
        elif outs[q].dtype == jnp.float32:
            total = outs[q][...] + part
        else:
            total = total + part
        last = n + 1 == len(blocks) or blocks[n + 1][0] != q
        if last or outs[q].dtype == jnp.float32:
            outs[q][...] = total.astype(outs[q].dtype)


def add_terms(scalars, queries, keys, totals=None, pairs=None, dtype=jnp.float32):
    if pairs is None:
        pairs = tuple(tuple((k, False) for k in range(len(keys))) for _ in queries)
    rows, width = queries[0].shape
    blocks = sum(len(p) for p in pairs)
    vmem = pl.BlockSpec(memory_space=pltpu.VMEM)
    arguments = (scalars, *queries, *keys, *(totals or ()))
    return pl.pallas_call(
        functools.partial(terms_kernel, pairs, len(queries), len(keys), totals is not None),
        out_shape=[jax.ShapeDtypeStruct((rows, width), dtype) for _ in queries],
        in_specs=[pl.BlockSpec(memory_space=pltpu.SMEM)] + [vmem] * (len(arguments) - 1),
        out_specs=[vmem] * len(queries),
        compiler_params=pltpu.CompilerParams(vmem_limit_bytes=16 * 1024 * 1024),
        cost_estimate=pl.CostEstimate(
            flops=4 * blocks * rows * rows * width,
            bytes_accessed=2 * rows * width * (len(queries) * 5 + len(keys)),
            transcendentals=blocks * rows * rows,
        ),
    )(*arguments)


def shards(images, texts, learned_sharpness, learned_offset_entry):
    scalars = jnp.concatenate([learned_sharpness, learned_offset_entry])
    first = lax.axis_index("member") % CORES == 0
    key = jnp.where(first, texts, images)
    query = jnp.where(first, images, texts)

    key_b = move(query, core=1)
    query_b = move(key, core=1)

    terms = functools.partial(add_terms, scalars)
    own, lent = (query, query_b), ()
    lent_a = move(query, column=1)
    a = move(key, ring=1), move(key, ring=-1)
    b = move(key_b, ring=1), move(key_b, ring=-1)
    total = terms(own, (key, key_b), pairs=(((0, True), (1, False)), ((0, False), (1, True))))

    (*a1, lent_a, _), total = wait((*a, lent_a, query_b), total)
    lent_b = move(after(key, a1), column=1, core=1)
    a = move(a1[0], ring=1), move(a1[1], ring=-1)
    total = terms(own, a1, total)

    b1, total = wait(b, total)
    b = move(b1[0], ring=1), move(b1[1], ring=-1)
    total = terms(own, b1, total)

    (*a2, lent_b), total = wait((*a, lent_b), total)
    near_a = move(after(key, a2), group=(1, -1))
    a = move(a2[0], ring=1), move(a2[1], ring=-1)
    lent = (lent_a, lent_b)
    loan = terms(lent, (key, key_b, *a1, *b1))

    b2, loan = wait(b, loan)
    b = move(b2[0], ring=1), move(b2[1], ring=-1)
    *total, loan_a, loan_b = terms((*own, *lent), a2, (*total, *loan))
    loan = loan_a, loan_b

    (*a3, near_a), loan = wait((*a, near_a), loan)
    a4 = move(a3[0], ring=1)
    near_b = move(after(query, a3), group=(-1, 1), core=1)
    *total, loan_a, loan_b = terms((*own, *lent), b2, (*total, *loan))
    loan = loan_a, loan_b

    b3_left, loan = wait(b[1], loan)
    b4 = move(b3_left, ring=-1)
    total = terms(own, a3, total)
    (b3_right, b3_left), total = wait((b[0], b3_left), total)
    loan = terms(lent, (*a3, b3_right, b3_left), loan)
    total = terms(own, (b3_right, b3_left), after(total, loan))

    (last, near_b), total, loan = lax.optimization_barrier((((a4, b4), near_b), total, loan))
    loan_a = terms(lent[:1], last, loan[:1], dtype=RETURN_TYPE)
    back_a = move(loan_a[0], column=1)
    loan_b = terms(lent[1:], last, after(loan[1:], loan_a), dtype=RETURN_TYPE)
    back_b = move(loan_b[0], column=1, core=1)
    own_b = terms(own[1:], (*last, near_b), after(total[1:], loan_b))
    other = jnp.concatenate([move(own_b[0][rows], core=1) for rows in THIRDS], axis=0)
    own_a = terms(own[:1], (*last, near_a), after(total[:1], own_b))

    mine = own_a[0] + back_a.astype(jnp.float32)
    other = other + back_b.astype(jnp.float32)
    return jnp.where(first, mine, other), jnp.where(first, other, mine)


def solution(mesh):
    rows = P(("group", "member"), None)
    return jax.shard_map(
        shards, mesh=mesh, in_specs=(rows, rows, P(), P()), out_specs=(rows, rows), check_vma=False
    )
```

```python
import functools

import jax
import jax.numpy as jnp
from jax import lax
from jax.experimental import pallas as pl
from jax.experimental.pallas import tpu as pltpu
from jax.sharding import PartitionSpec as P

GROUPS, COLUMNS, RING, CORES = 8, 2, 8, 2
MEMBERS = COLUMNS * RING * CORES
RETURN_TYPE = jnp.bfloat16
THIRDS = slice(0, 96), slice(96, 192), slice(192, 256)


def move(rows, group=0, column=0, ring=0, core=0, only=None):
    pairs = []
    by_core = group if isinstance(group, tuple) else (group, group)
    for g in range(GROUPS):
        for y in range(COLUMNS):
            for z in range(RING):
                for c in range(CORES) if only is None else (only,):
                    here = ((g * COLUMNS + y) * RING + z) * CORES + c
                    there = (g + by_core[c]) % GROUPS
                    there = there * COLUMNS + (y + column) % COLUMNS
                    there = there * RING + (z + ring) % RING
                    there = there * CORES + (c + core) % CORES
                    pairs.append((here, there))
    return lax.ppermute(rows, ("group", "member"), pairs)


def after(rows, event):
    return lax.optimization_barrier((rows, event))[0]


def wait(arriving, totals):
    return lax.optimization_barrier((arriving, totals))


def weights(scores, sharpness, offset, diagonal):
    logits = sharpness * scores + offset
    if not diagonal:
        return (sharpness / (1.0 + jnp.exp(-logits))).astype(jnp.bfloat16)
    rows = lax.broadcasted_iota(jnp.int32, logits.shape, 0)
    columns = lax.broadcasted_iota(jnp.int32, logits.shape, 1)
    polarity = jnp.where(rows == columns, 1.0, -1.0).astype(jnp.float32)
    return (-sharpness * polarity / (1.0 + jnp.exp(polarity * logits))).astype(jnp.bfloat16)


def terms_kernel(pairs, n_queries, n_keys, has_total, scalars, *refs):
    queries = refs[:n_queries]
    keys = refs[n_queries : n_queries + n_keys]
    totals = refs[n_queries + n_keys : len(refs) - n_queries] if has_total else ()
    outs = refs[len(refs) - n_queries :]
    sharpness, offset = scalars[0], scalars[1]
    blocks = [(q, k, diagonal) for q in range(n_queries) for k, diagonal in pairs[q]]

    def scores(q, k):
        contract = (((1,), (1,)), ((), ()))
        return lax.dot_general(queries[q][...], keys[k][...], contract, preferred_element_type=jnp.float32)

    total, ahead = None, scores(*blocks[0][:2])
    for n, (q, k, diagonal) in enumerate(blocks):
        now, ahead = ahead, scores(*blocks[n + 1][:2]) if n + 1 < len(blocks) else None
        part = jnp.dot(
            weights(now, sharpness, offset, diagonal), keys[k][...], preferred_element_type=jnp.float32
        )
        if n == 0 or blocks[n - 1][0] != q:
            total = totals[q][...] + part if has_total else part
        elif outs[q].dtype == jnp.float32:
            total = outs[q][...] + part
        else:
            total = total + part
        last = n + 1 == len(blocks) or blocks[n + 1][0] != q
        if last or outs[q].dtype == jnp.float32:
            outs[q][...] = total.astype(outs[q].dtype)


def add_terms(scalars, queries, keys, totals=None, pairs=None, dtype=jnp.float32):
    if pairs is None:
        pairs = tuple(tuple((k, False) for k in range(len(keys))) for _ in queries)
    rows, width = queries[0].shape
    blocks = sum(len(p) for p in pairs)
    vmem = pl.BlockSpec(memory_space=pltpu.VMEM)
    arguments = (scalars, *queries, *keys, *(totals or ()))
    return pl.pallas_call(
        functools.partial(terms_kernel, pairs, len(queries), len(keys), totals is not None),
        out_shape=[jax.ShapeDtypeStruct((rows, width), dtype) for _ in queries],
        in_specs=[pl.BlockSpec(memory_space=pltpu.SMEM)] + [vmem] * (len(arguments) - 1),
        out_specs=[vmem] * len(queries),
        compiler_params=pltpu.CompilerParams(vmem_limit_bytes=16 * 1024 * 1024),
        cost_estimate=pl.CostEstimate(
            flops=4 * blocks * rows * rows * width,
            bytes_accessed=2 * rows * width * (len(queries) * 5 + len(keys)),
            transcendentals=blocks * rows * rows,
        ),
    )(*arguments)


def shards(images, texts, learned_sharpness, learned_offset_entry):
    scalars = jnp.concatenate([learned_sharpness, learned_offset_entry])
    first = lax.axis_index("member") % CORES == 0
    key = jnp.where(first, texts, images)
    query = jnp.where(first, images, texts)

    key_b = move(query, core=1)
    query_b = move(key, core=1)

    terms = functools.partial(add_terms, scalars)
    own, lent = (query, query_b), ()
    lent_a = move(query, column=1)
    a = move(key, ring=1), move(key, ring=-1)
    b = move(key_b, ring=1), move(key_b, ring=-1)
    total = terms(own, (key, key_b), pairs=(((0, True), (1, False)), ((0, False), (1, True))))

    (*a1, lent_a, _), total = wait((*a, lent_a, query_b), total)
    lent_b = move(after(key, a1), column=1, core=1)
    a = move(a1[0], ring=1), move(a1[1], ring=-1)
    total = terms(own, a1, total)

    b1, total = wait(b, total)
    b = move(b1[0], ring=1), move(b1[1], ring=-1)
    total = terms(own, b1, total)

    (*a2, lent_b), total = wait((*a, lent_b), total)
    a = move(a2[0], ring=1), move(a2[1], ring=-1)
    lent = (lent_a, lent_b)
    loan = terms(lent, (key, key_b, *a1))

    b2, loan = wait(b, loan)
    b = move(b2[0], ring=1), move(b2[1], ring=-1)
    near_a = move(after(key, b2), group=(1, -1))
    *total, loan_a, loan_b = terms(
        (*own, *lent),
        (*a2, *b1),
        (*total, *loan),
        tuple(tuple((k, False) for k in range(n)) for n in (2, 2, 4, 4)),
    )
    loan = loan_a, loan_b

    a3, loan = wait(a, loan)
    a4 = move(a3[0], ring=1, only=0)
    near_b = move(after(query, a3), group=(-1, 1), core=1)
    *total, loan_a, loan_b = terms((*own, *lent), b2, (*total, *loan))
    loan = loan_a, loan_b
    a4_second = move(after(a3[0], loan), ring=1, only=1)

    b3_left, loan = wait(b[1], loan)
    b4 = move(b3_left, ring=-1, only=0)
    total = terms(own, a3, total)
    (b3_right, b3_left, near_a), total = wait((b[0], b3_left, near_a), total)
    b4_second = move(b3_left, ring=-1, only=1)
    loan = terms(lent, (*a3, b3_right, b3_left), loan)
    total = terms(own, (b3_right, b3_left), after(total, loan))

    (a4, b4, near_b), total, loan = lax.optimization_barrier(((a4, b4, near_b), total, loan))
    loan_b = terms(lent[1:], (a4, b4), loan[1:], dtype=RETURN_TYPE)
    back_b = move(loan_b[0], column=1, core=1, only=0)
    loan_a = terms(lent[:1], (a4, b4), after(loan[:1], loan_b), dtype=RETURN_TYPE)
    back_a = move(loan_a[0], column=1, only=0)
    last, loan, back_b = lax.optimization_barrier(((a4_second, b4_second), after(loan, loan_a), back_b))
    loan_a = terms(lent[:1], last, loan[:1], dtype=RETURN_TYPE)
    back_a_second = move(loan_a[0], column=1, only=1)
    loan_b = terms(lent[1:], last, after(loan[1:], loan_a), dtype=RETURN_TYPE)
    back_b_second = move(loan_b[0], column=1, core=1, only=1)
    total, back_a = lax.optimization_barrier((after(total, loan_b), back_a))
    own_b = terms(own[1:], (a4, b4, *last, near_b), total[1:])
    other = jnp.concatenate([move(own_b[0][rows], core=1) for rows in THIRDS], axis=0)
    own_a = terms(own[:1], (a4, b4, *last, near_a), after(total[:1], own_b))

    mine = own_a[0] + back_a.astype(jnp.float32) + back_a_second.astype(jnp.float32)
    other = other + back_b.astype(jnp.float32) + back_b_second.astype(jnp.float32)
    return jnp.where(first, mine, other), jnp.where(first, other, mine)


def solution(mesh):
    rows = P(("group", "member"), None)
    return jax.shard_map(
        shards, mesh=mesh, in_specs=(rows, rows, P(), P()), out_specs=(rows, rows), check_vma=False
    )
```

```python
import functools

import jax
import jax.numpy as jnp
from jax import lax
from jax.experimental import pallas as pl
from jax.experimental.pallas import tpu as pltpu
from jax.sharding import PartitionSpec as P

GROUPS, COLUMNS, RING, CORES, ROWS = 8, 2, 8, 2, 256
MEMBERS = COLUMNS * RING * CORES
RETURN_TYPE = jnp.bfloat16
THIRDS = slice(0, 96), slice(96, 192), slice(192, 256)


def move(rows, group=0, column=0, ring=0, core=0):
    pairs = []
    by_core = group if isinstance(group, tuple) else (group, group)
    for g in range(GROUPS):
        for y in range(COLUMNS):
            for z in range(RING):
                for c in range(CORES):
                    here = ((g * COLUMNS + y) * RING + z) * CORES + c
                    there = (g + by_core[c]) % GROUPS
                    there = there * COLUMNS + (y + column) % COLUMNS
                    there = there * RING + (z + ring) % RING
                    there = there * CORES + (c + core) % CORES
                    pairs.append((here, there))
    return lax.ppermute(rows, ("group", "member"), pairs)


def after(rows, event):
    return lax.optimization_barrier((rows, event))[0]


def wait(arriving, totals):
    return lax.optimization_barrier((arriving, totals))


def weights(scores, sharpness, offset, diagonal):
    logits = sharpness * scores + offset
    if not diagonal:
        return (sharpness / (1.0 + jnp.exp(-logits))).astype(jnp.bfloat16)
    rows = lax.broadcasted_iota(jnp.int32, logits.shape, 0)
    columns = lax.broadcasted_iota(jnp.int32, logits.shape, 1)
    polarity = jnp.where(rows == columns, 1.0, -1.0).astype(jnp.float32)
    return (-sharpness * polarity / (1.0 + jnp.exp(polarity * logits))).astype(jnp.bfloat16)


def terms_kernel(pairs, starts, n_queries, n_keys, has_total, scalars, *refs):
    blocks = [ref.at[pl.ds(start, refs[-1].shape[0])] for ref, start in zip(refs, starts)]
    queries = blocks[:n_queries]
    keys = blocks[n_queries:]
    totals = refs[n_queries + n_keys : len(refs) - n_queries] if has_total else ()
    outs = refs[len(refs) - n_queries :]
    sharpness, offset = scalars[0], scalars[1]
    blocks = [(q, k, diagonal) for q in range(n_queries) for k, diagonal in pairs[q]]

    def scores(q, k):
        contract = (((1,), (1,)), ((), ()))
        return lax.dot_general(queries[q][...], keys[k][...], contract, preferred_element_type=jnp.float32)

    total, ahead = None, scores(*blocks[0][:2])
    for n, (q, k, diagonal) in enumerate(blocks):
        now, ahead = ahead, scores(*blocks[n + 1][:2]) if n + 1 < len(blocks) else None
        part = jnp.dot(
            weights(now, sharpness, offset, diagonal), keys[k][...], preferred_element_type=jnp.float32
        )
        if n == 0 or blocks[n - 1][0] != q:
            total = totals[q][...] + part if has_total else part
        elif outs[q].dtype == jnp.float32:
            total = outs[q][...] + part
        else:
            total = total + part
        last = n + 1 == len(blocks) or blocks[n + 1][0] != q
        if last or outs[q].dtype == jnp.float32:
            outs[q][...] = total.astype(outs[q].dtype)


def add_terms(scalars, queries, keys, totals=None, pairs=None, dtype=jnp.float32):
    if pairs is None:
        pairs = tuple(tuple((k, False) for k in range(len(keys))) for _ in queries)
    arrays = [block if isinstance(block, tuple) else (block, 0) for block in (*queries, *keys)]
    arrays, starts = zip(*arrays)
    rows, width = ROWS, arrays[0].shape[1]
    blocks = sum(len(p) for p in pairs)
    vmem = pl.BlockSpec(memory_space=pltpu.VMEM)
    arguments = (scalars, *arrays, *(totals or ()))
    return pl.pallas_call(
        functools.partial(terms_kernel, pairs, starts, len(queries), len(keys), totals is not None),
        out_shape=[jax.ShapeDtypeStruct((rows, width), dtype) for _ in queries],
        in_specs=[pl.BlockSpec(memory_space=pltpu.SMEM)] + [vmem] * (len(arguments) - 1),
        out_specs=[vmem] * len(queries),
        compiler_params=pltpu.CompilerParams(vmem_limit_bytes=16 * 1024 * 1024),
        cost_estimate=pl.CostEstimate(
            flops=4 * blocks * rows * rows * width,
            bytes_accessed=2 * rows * width * (len(queries) * 5 + len(keys)),
            transcendentals=blocks * rows * rows,
        ),
    )(*arguments)


def shards(images, texts, learned_sharpness, learned_offset_entry):
    scalars = jnp.concatenate([learned_sharpness, learned_offset_entry])
    first = lax.axis_index("member") % CORES == 0
    key = jnp.where(first, texts, images)
    query = jnp.where(first, images, texts)

    key_b = move(query, core=1)
    query_b = move(key, core=1)

    terms = functools.partial(add_terms, scalars)
    a = move(key, ring=1), move(key, ring=-1)
    b = move(key_b, ring=1), move(key_b, ring=-1)
    own = (query, query_b)
    total = terms(own, (key, key_b), pairs=(((0, True), (1, False)), ((0, False), (1, True))))

    a1, total = wait(a, total)
    a = move(a1[0], ring=1), move(a1[1], ring=-1)
    lent = move(jnp.concatenate([query, query_b]), column=1)
    total = terms(own, a1, total)

    b1, total = wait(b, total)
    b = move(b1[0], ring=1), move(b1[1], ring=-1)
    total = terms(own, b1, total)

    (*a2, lent), total = wait((*a, lent), total)
    a = move(a2[0], ring=1), move(a2[1], ring=-1)
    near = move(after(jnp.concatenate([key, key_b]), a2), group=(1, -1))
    lent = (lent, 0), (lent, ROWS)
    loan = terms(lent, (key, key_b, *a1, *b1))

    b2, loan = wait(b, loan)
    b = move(b2[0], ring=1), move(b2[1], ring=-1)
    *total, loan_a, loan_b = terms((*own, *lent), a2, (*total, *loan))
    loan = loan_a, loan_b

    a3, loan = wait(a, loan)
    a4 = move(a3[0], ring=1)
    *total, loan_a, loan_b = terms((*own, *lent), b2, (*total, *loan))
    loan = loan_a, loan_b

    b3_left, loan = wait(b[1], loan)
    b4 = move(b3_left, ring=-1)
    total = terms(own, a3, total)
    (b3_right, b3_left, near), total = wait((b[0], b3_left, near), total)
    loan = terms(lent, (*a3, b3_right, b3_left), loan)
    a4, loan = wait(a4, loan)
    *total, loan_a, loan_b = terms(
        (*own, *lent),
        (b3_right, b3_left, a4),
        (*total, *loan),
        tuple(tuple((k, False) for k in keys) for keys in ((0, 1), (0, 1), (2,), (2,))),
    )

    b4, total, loan = lax.optimization_barrier((b4, total, (loan_a, loan_b)))
    last = a4, b4
    loan_a = terms(lent[:1], (b4,), loan[:1], dtype=RETURN_TYPE)
    back_a = move(loan_a[0], column=1)
    loan_b = terms(lent[1:], (b4,), after(loan[1:], loan_a), dtype=RETURN_TYPE)
    back_b = move(loan_b[0], column=1, core=1)
    own_b = terms(own[1:], (*last, (near, ROWS)), after(total[1:], loan_b))
    other = jnp.concatenate([move(own_b[0][rows], core=1) for rows in THIRDS], axis=0)
    own_a = terms(own[:1], (*last, (near, 0)), after(total[:1], own_b))

    mine = own_a[0] + back_a.astype(jnp.float32)
    other = other + back_b.astype(jnp.float32)
    return jnp.where(first, mine, other), jnp.where(first, other, mine)


def solution(mesh):
    rows = P(("group", "member"), None)
    return jax.shard_map(
        shards, mesh=mesh, in_specs=(rows, rows, P(), P()), out_specs=(rows, rows), check_vma=False
    )
```

```python
import functools

import jax
import jax.numpy as jnp
from jax import lax
from jax.experimental import pallas as pl
from jax.experimental.pallas import tpu as pltpu
from jax.sharding import PartitionSpec as P

GROUPS, COLUMNS, RING, CORES, ROWS = 8, 2, 8, 2, 256
MEMBERS = COLUMNS * RING * CORES
RETURN_TYPE = jnp.bfloat16
THIRDS = slice(0, 96), slice(96, 192), slice(192, 256)


def move(rows, group=0, column=0, ring=0, core=0, only=None):
    pairs = []
    by_core = group if isinstance(group, tuple) else (group, group)
    for g in range(GROUPS):
        for y in range(COLUMNS):
            for z in range(RING):
                for c in range(CORES) if only is None else (only,):
                    here = ((g * COLUMNS + y) * RING + z) * CORES + c
                    there = (g + by_core[c]) % GROUPS
                    there = there * COLUMNS + (y + column) % COLUMNS
                    there = there * RING + (z + ring) % RING
                    there = there * CORES + (c + core) % CORES
                    pairs.append((here, there))
    return lax.ppermute(rows, ("group", "member"), pairs)


def after(rows, event):
    return lax.optimization_barrier((rows, event))[0]


def wait(arriving, totals):
    return lax.optimization_barrier((arriving, totals))


def weights(scores, sharpness, offset, diagonal):
    logits = sharpness * scores + offset
    if not diagonal:
        return (sharpness / (1.0 + jnp.exp(-logits))).astype(jnp.bfloat16)
    rows = lax.broadcasted_iota(jnp.int32, logits.shape, 0)
    columns = lax.broadcasted_iota(jnp.int32, logits.shape, 1)
    polarity = jnp.where(rows == columns, 1.0, -1.0).astype(jnp.float32)
    return (-sharpness * polarity / (1.0 + jnp.exp(polarity * logits))).astype(jnp.bfloat16)


def terms_kernel(pairs, starts, n_queries, n_keys, has_total, scalars, *refs):
    blocks = [ref.at[pl.ds(start, refs[-1].shape[0])] for ref, start in zip(refs, starts)]
    queries = blocks[:n_queries]
    keys = blocks[n_queries:]
    totals = refs[n_queries + n_keys : len(refs) - n_queries] if has_total else ()
    outs = refs[len(refs) - n_queries :]
    sharpness, offset = scalars[0], scalars[1]
    blocks = [(q, k, diagonal) for q in range(n_queries) for k, diagonal in pairs[q]]

    def scores(q, k):
        contract = (((1,), (1,)), ((), ()))
        return lax.dot_general(queries[q][...], keys[k][...], contract, preferred_element_type=jnp.float32)

    total, ahead = None, scores(*blocks[0][:2])
    for n, (q, k, diagonal) in enumerate(blocks):
        now, ahead = ahead, scores(*blocks[n + 1][:2]) if n + 1 < len(blocks) else None
        part = jnp.dot(
            weights(now, sharpness, offset, diagonal), keys[k][...], preferred_element_type=jnp.float32
        )
        if n == 0 or blocks[n - 1][0] != q:
            total = totals[q][...] + part if has_total else part
        elif outs[q].dtype == jnp.float32:
            total = outs[q][...] + part
        else:
            total = total + part
        last = n + 1 == len(blocks) or blocks[n + 1][0] != q
        if last or outs[q].dtype == jnp.float32:
            outs[q][...] = total.astype(outs[q].dtype)


def add_terms(scalars, queries, keys, totals=None, pairs=None, dtype=jnp.float32):
    if pairs is None:
        pairs = tuple(tuple((k, False) for k in range(len(keys))) for _ in queries)
    arrays = [block if isinstance(block, tuple) else (block, 0) for block in (*queries, *keys)]
    arrays, starts = zip(*arrays)
    rows, width = ROWS, arrays[0].shape[1]
    blocks = sum(len(p) for p in pairs)
    vmem = pl.BlockSpec(memory_space=pltpu.VMEM)
    arguments = (scalars, *arrays, *(totals or ()))
    return pl.pallas_call(
        functools.partial(terms_kernel, pairs, starts, len(queries), len(keys), totals is not None),
        out_shape=[jax.ShapeDtypeStruct((rows, width), dtype) for _ in queries],
        in_specs=[pl.BlockSpec(memory_space=pltpu.SMEM)] + [vmem] * (len(arguments) - 1),
        out_specs=[vmem] * len(queries),
        compiler_params=pltpu.CompilerParams(vmem_limit_bytes=16 * 1024 * 1024),
        cost_estimate=pl.CostEstimate(
            flops=4 * blocks * rows * rows * width,
            bytes_accessed=2 * rows * width * (len(queries) * 5 + len(keys)),
            transcendentals=blocks * rows * rows,
        ),
    )(*arguments)


def shards(images, texts, learned_sharpness, learned_offset_entry):
    scalars = jnp.concatenate([learned_sharpness, learned_offset_entry])
    first = lax.axis_index("member") % CORES == 0
    key = jnp.where(first, texts, images)
    query = jnp.where(first, images, texts)

    key_b = move(query, core=1)
    query_b = move(key, core=1)

    terms = functools.partial(add_terms, scalars)
    a = move(key, ring=1), move(key, ring=-1)
    b = move(key_b, ring=1), move(key_b, ring=-1)
    own = (query, query_b)
    total = terms(own, (key, key_b), pairs=(((0, True), (1, False)), ((0, False), (1, True))))

    a1, total = wait(a, total)
    a = move(a1[0], ring=1), move(a1[1], ring=-1)
    lent = move(jnp.concatenate([query, query_b]), column=1)
    total = terms(own, a1, total)

    b1, total = wait(b, total)
    b = move(b1[0], ring=1), move(b1[1], ring=-1)
    total = terms(own, b1, total)

    (*a2, lent), total = wait((*a, lent), total)
    a = move(a2[0], ring=1), move(a2[1], ring=-1)
    near = move(after(jnp.concatenate([key, key_b]), a2), group=(1, -1))
    lent = (lent, 0), (lent, ROWS)
    loan = terms(lent, (key, key_b, *a1, *b1))

    b2, loan = wait(b, loan)
    b = move(b2[0], ring=1), move(b2[1], ring=-1)
    *total, loan_a, loan_b = terms((*own, *lent), a2, (*total, *loan))
    loan = loan_a, loan_b

    a3, loan = wait(a, loan)
    a4 = move(a3[0], ring=1, only=0)
    *total, loan_a, loan_b = terms((*own, *lent), b2, (*total, *loan))
    loan = loan_a, loan_b
    a4_second = move(after(a3[0], loan), ring=1, only=1)

    b3_left, (loan, total) = wait(b[1], (loan, total))
    b4 = move(b3_left, ring=-1, only=0)
    total = terms(own, a3, total)
    (b3_right, b3_left, near), total = wait((b[0], b3_left, near), total)
    b4_second = move(b3_left, ring=-1, only=1)
    loan = terms(lent, (*a3, b3_right, b3_left), loan)

    last, total, loan = lax.optimization_barrier(((a4, b4, a4_second, b4_second), total, loan))
    loan_a = terms(lent[:1], last, loan[:1], dtype=RETURN_TYPE)
    back_a = move(loan_a[0], column=1)
    loan_b = terms(lent[1:], last, after(loan[1:], loan_a), dtype=RETURN_TYPE)
    back_b = move(loan_b[0], column=1, core=1)
    rest = b3_right, b3_left, *last
    own_b = terms(own[1:], (*rest, (near, ROWS)), after(total[1:], loan_b))
    other = jnp.concatenate([move(own_b[0][rows], core=1) for rows in THIRDS], axis=0)
    own_a = terms(own[:1], (*rest, (near, 0)), after(total[:1], own_b))

    mine = own_a[0] + back_a.astype(jnp.float32)
    other = other + back_b.astype(jnp.float32)
    return jnp.where(first, mine, other), jnp.where(first, other, mine)


def solution(mesh):
    rows = P(("group", "member"), None)
    return jax.shard_map(
        shards, mesh=mesh, in_specs=(rows, rows, P(), P()), out_specs=(rows, rows), check_vma=False
    )
```

```python
import functools

import jax
import jax.numpy as jnp
from jax import lax
from jax.experimental import pallas as pl
from jax.experimental.pallas import tpu as pltpu
from jax.sharding import PartitionSpec as P

GROUPS, COLUMNS, RING, CORES, ROWS = 8, 2, 8, 2, 256
MEMBERS = COLUMNS * RING * CORES
RETURN_TYPE = jnp.bfloat16
THIRDS = slice(0, 96), slice(96, 192), slice(192, 256)


def move(rows, group=0, column=0, ring=0, core=0):
    pairs = []
    by_core = group if isinstance(group, tuple) else (group, group)
    for g in range(GROUPS):
        for y in range(COLUMNS):
            for z in range(RING):
                for c in range(CORES):
                    here = ((g * COLUMNS + y) * RING + z) * CORES + c
                    there = (g + by_core[c]) % GROUPS
                    there = there * COLUMNS + (y + column) % COLUMNS
                    there = there * RING + (z + ring) % RING
                    there = there * CORES + (c + core) % CORES
                    pairs.append((here, there))
    return lax.ppermute(rows, ("group", "member"), pairs)


def after(rows, event):
    return lax.optimization_barrier((rows, event))[0]


def wait(arriving, totals):
    return lax.optimization_barrier((arriving, totals))


def weights(scores, sharpness, offset, diagonal):
    logits = sharpness * scores + offset
    if not diagonal:
        return (sharpness / (1.0 + jnp.exp(-logits))).astype(jnp.bfloat16)
    rows = lax.broadcasted_iota(jnp.int32, logits.shape, 0)
    columns = lax.broadcasted_iota(jnp.int32, logits.shape, 1)
    polarity = jnp.where(rows == columns, 1.0, -1.0).astype(jnp.float32)
    return (-sharpness * polarity / (1.0 + jnp.exp(polarity * logits))).astype(jnp.bfloat16)


def terms_kernel(pairs, starts, n_queries, n_keys, has_total, scalars, *refs):
    blocks = [ref.at[pl.ds(start, refs[-1].shape[0])] for ref, start in zip(refs, starts)]
    queries = blocks[:n_queries]
    keys = blocks[n_queries:]
    totals = refs[n_queries + n_keys : len(refs) - n_queries] if has_total else ()
    outs = refs[len(refs) - n_queries :]
    sharpness, offset = scalars[0], scalars[1]
    blocks = [(q, k, diagonal) for q in range(n_queries) for k, diagonal in pairs[q]]

    def scores(q, k):
        contract = (((1,), (1,)), ((), ()))
        return lax.dot_general(queries[q][...], keys[k][...], contract, preferred_element_type=jnp.float32)

    total, ahead = None, scores(*blocks[0][:2])
    for n, (q, k, diagonal) in enumerate(blocks):
        now, ahead = ahead, scores(*blocks[n + 1][:2]) if n + 1 < len(blocks) else None
        part = jnp.dot(
            weights(now, sharpness, offset, diagonal), keys[k][...], preferred_element_type=jnp.float32
        )
        if n == 0 or blocks[n - 1][0] != q:
            total = totals[q][...] + part if has_total else part
        elif outs[q].dtype == jnp.float32:
            total = outs[q][...] + part
        else:
            total = total + part
        last = n + 1 == len(blocks) or blocks[n + 1][0] != q
        if last or outs[q].dtype == jnp.float32:
            outs[q][...] = total.astype(outs[q].dtype)


def add_terms(scalars, queries, keys, totals=None, pairs=None, dtype=jnp.float32):
    if pairs is None:
        pairs = tuple(tuple((k, False) for k in range(len(keys))) for _ in queries)
    arrays = [block if isinstance(block, tuple) else (block, 0) for block in (*queries, *keys)]
    arrays, starts = zip(*arrays)
    rows, width = ROWS, arrays[0].shape[1]
    blocks = sum(len(p) for p in pairs)
    vmem = pl.BlockSpec(memory_space=pltpu.VMEM)
    arguments = (scalars, *arrays, *(totals or ()))
    return pl.pallas_call(
        functools.partial(terms_kernel, pairs, starts, len(queries), len(keys), totals is not None),
        out_shape=[jax.ShapeDtypeStruct((rows, width), dtype) for _ in queries],
        in_specs=[pl.BlockSpec(memory_space=pltpu.SMEM)] + [vmem] * (len(arguments) - 1),
        out_specs=[vmem] * len(queries),
        compiler_params=pltpu.CompilerParams(vmem_limit_bytes=16 * 1024 * 1024),
        cost_estimate=pl.CostEstimate(
            flops=4 * blocks * rows * rows * width,
            bytes_accessed=2 * rows * width * (len(queries) * 5 + len(keys)),
            transcendentals=blocks * rows * rows,
        ),
    )(*arguments)


def shards(images, texts, learned_sharpness, learned_offset_entry):
    scalars = jnp.concatenate([learned_sharpness, learned_offset_entry])
    first = lax.axis_index("member") % CORES == 0
    key = jnp.where(first, texts, images)
    query = jnp.where(first, images, texts)

    key_b = move(query, core=1)
    query_b = move(key, core=1)

    terms = functools.partial(add_terms, scalars)
    a = move(key, ring=1), move(key, ring=-1)
    b = move(key_b, ring=1), move(key_b, ring=-1)
    own = (query, query_b)
    total = terms(own, (key, key_b), pairs=(((0, True), (1, False)), ((0, False), (1, True))))

    a1, total = wait(a, total)
    a = move(a1[0], ring=1), move(a1[1], ring=-1)
    lent = move(jnp.concatenate([query, query_b]), column=1)
    total = terms(own, a1, total)

    b1, total = wait(b, total)
    b = move(b1[0], ring=1), move(b1[1], ring=-1)
    total = terms(own, b1, total)

    (*a2, lent), total = wait((*a, lent), total)
    a = move(a2[0], ring=1), move(a2[1], ring=-1)
    lent = (lent, 0), (lent, ROWS)
    loan = terms(lent, (key, key_b, *a1, *b1))

    b2, loan = wait(b, loan)
    b = move(b2[0], ring=1), move(b2[1], ring=-1)
    near = move(after(jnp.concatenate([key, key_b]), b2), group=(1, -1))
    *total, loan_a, loan_b = terms((*own, *lent), a2, (*total, *loan))
    loan = loan_a, loan_b

    a3, loan = wait(a, loan)
    a4 = move(a3[0], ring=1)
    *total, loan_a, loan_b = terms((*own, *lent), b2, (*total, *loan))
    loan = loan_a, loan_b

    b3_left, loan = wait(b[1], loan)
    b4 = move(b3_left, ring=-1)
    total = terms(own, a3, total)
    (b3_right, b3_left), total = wait((b[0], b3_left), total)
    loan = terms(lent, (*a3, b3_right, b3_left), loan)
    a4, loan = wait(a4, loan)
    *total, loan_a, loan_b = terms(
        (*own, *lent),
        (b3_right, b3_left, a4),
        (*total, *loan),
        tuple(tuple((k, False) for k in keys) for keys in ((0, 1), (0, 1), (2,), (2,))),
    )

    (b4, near), total, loan = lax.optimization_barrier(((b4, near), total, (loan_a, loan_b)))
    last = a4, b4
    loan_a = terms(lent[:1], (b4,), loan[:1], dtype=RETURN_TYPE)
    back_a = move(loan_a[0], column=1)
    loan_b = terms(lent[1:], (b4,), after(loan[1:], loan_a), dtype=RETURN_TYPE)
    back_b = move(loan_b[0], column=1, core=1)
    own_b = terms(own[1:], (*last, (near, ROWS)), after(total[1:], loan_b))
    other = jnp.concatenate([move(own_b[0][rows], core=1) for rows in THIRDS], axis=0)
    own_a = terms(own[:1], (*last, (near, 0)), after(total[:1], own_b))

    mine = own_a[0] + back_a.astype(jnp.float32)
    other = other + back_b.astype(jnp.float32)
    return jnp.where(first, mine, other), jnp.where(first, other, mine)


def solution(mesh):
    rows = P(("group", "member"), None)
    return jax.shard_map(
        shards, mesh=mesh, in_specs=(rows, rows, P(), P()), out_specs=(rows, rows), check_vma=False
    )
```

```python
import functools

import jax
import jax.numpy as jnp
from jax import lax
from jax.experimental import pallas as pl
from jax.experimental.pallas import tpu as pltpu
from jax.sharding import PartitionSpec as P

GROUPS, COLUMNS, RING, CORES, ROWS = 8, 2, 8, 2, 256
MEMBERS = COLUMNS * RING * CORES
RETURN_TYPE = jnp.bfloat16
THIRDS = slice(0, 96), slice(96, 192), slice(192, 256)


def move(rows, group=0, column=0, ring=0, core=0):
    pairs = []
    by_core = group if isinstance(group, tuple) else (group, group)
    for g in range(GROUPS):
        for y in range(COLUMNS):
            for z in range(RING):
                for c in range(CORES):
                    here = ((g * COLUMNS + y) * RING + z) * CORES + c
                    there = (g + by_core[c]) % GROUPS
                    there = there * COLUMNS + (y + column) % COLUMNS
                    there = there * RING + (z + ring) % RING
                    there = there * CORES + (c + core) % CORES
                    pairs.append((here, there))
    return lax.ppermute(rows, ("group", "member"), pairs)


def after(rows, event):
    return lax.optimization_barrier((rows, event))[0]


def wait(arriving, totals):
    return lax.optimization_barrier((arriving, totals))


def weights(scores, sharpness, offset, diagonal):
    logits = sharpness * scores + offset
    if not diagonal:
        return (sharpness / (1.0 + jnp.exp(-logits))).astype(jnp.bfloat16)
    rows = lax.broadcasted_iota(jnp.int32, logits.shape, 0)
    columns = lax.broadcasted_iota(jnp.int32, logits.shape, 1)
    polarity = jnp.where(rows == columns, 1.0, -1.0).astype(jnp.float32)
    return (-sharpness * polarity / (1.0 + jnp.exp(polarity * logits))).astype(jnp.bfloat16)


def terms_kernel(pairs, starts, n_queries, n_keys, has_total, scalars, *refs):
    blocks = [ref.at[pl.ds(start, refs[-1].shape[0])] for ref, start in zip(refs, starts)]
    queries = blocks[:n_queries]
    keys = blocks[n_queries:]
    totals = refs[n_queries + n_keys : len(refs) - n_queries] if has_total else ()
    outs = refs[len(refs) - n_queries :]
    sharpness, offset = scalars[0], scalars[1]
    blocks = [(q, k, diagonal) for q in range(n_queries) for k, diagonal in pairs[q]]

    def scores(q, k):
        contract = (((1,), (1,)), ((), ()))
        return lax.dot_general(queries[q][...], keys[k][...], contract, preferred_element_type=jnp.float32)

    total, ahead = None, scores(*blocks[0][:2])
    for n, (q, k, diagonal) in enumerate(blocks):
        now, ahead = ahead, scores(*blocks[n + 1][:2]) if n + 1 < len(blocks) else None
        part = jnp.dot(
            weights(now, sharpness, offset, diagonal), keys[k][...], preferred_element_type=jnp.float32
        )
        if n == 0 or blocks[n - 1][0] != q:
            total = totals[q][...] + part if has_total else part
        elif outs[q].dtype == jnp.float32:
            total = outs[q][...] + part
        else:
            total = total + part
        last = n + 1 == len(blocks) or blocks[n + 1][0] != q
        if last or outs[q].dtype == jnp.float32:
            outs[q][...] = total.astype(outs[q].dtype)


def add_terms(scalars, queries, keys, totals=None, pairs=None, dtype=jnp.float32):
    if pairs is None:
        pairs = tuple(tuple((k, False) for k in range(len(keys))) for _ in queries)
    arrays = [block if isinstance(block, tuple) else (block, 0) for block in (*queries, *keys)]
    arrays, starts = zip(*arrays)
    rows, width = ROWS, arrays[0].shape[1]
    blocks = sum(len(p) for p in pairs)
    vmem = pl.BlockSpec(memory_space=pltpu.VMEM)
    arguments = (scalars, *arrays, *(totals or ()))
    return pl.pallas_call(
        functools.partial(terms_kernel, pairs, starts, len(queries), len(keys), totals is not None),
        out_shape=[jax.ShapeDtypeStruct((rows, width), dtype) for _ in queries],
        in_specs=[pl.BlockSpec(memory_space=pltpu.SMEM)] + [vmem] * (len(arguments) - 1),
        out_specs=[vmem] * len(queries),
        compiler_params=pltpu.CompilerParams(vmem_limit_bytes=16 * 1024 * 1024),
        cost_estimate=pl.CostEstimate(
            flops=4 * blocks * rows * rows * width,
            bytes_accessed=2 * rows * width * (len(queries) * 5 + len(keys)),
            transcendentals=blocks * rows * rows,
        ),
    )(*arguments)


def shards(images, texts, learned_sharpness, learned_offset_entry):
    scalars = jnp.concatenate([learned_sharpness, learned_offset_entry])
    first = lax.axis_index("member") % CORES == 0
    key = jnp.where(first, texts, images)
    query = jnp.where(first, images, texts)

    key_b = move(query, core=1)
    query_b = move(key, core=1)

    terms = functools.partial(add_terms, scalars)
    a = move(key, ring=1), move(key, ring=-1)
    b = move(key_b, ring=1), move(key_b, ring=-1)
    own = (query, query_b)
    total = terms(own, (key, key_b), pairs=(((0, True), (1, False)), ((0, False), (1, True))))

    a1, total = wait(a, total)
    a = move(a1[0], ring=1), move(a1[1], ring=-1)
    lent = move(jnp.concatenate([query, query_b]), column=1)
    total = terms(own, a1, total)

    b1, total = wait(b, total)
    b = move(b1[0], ring=1), move(b1[1], ring=-1)
    total = terms(own, b1, total)

    (*a2, lent), total = wait((*a, lent), total)
    a = move(a2[0], ring=1), move(a2[1], ring=-1)
    lent = (lent, 0), (lent, ROWS)
    loan = terms(lent, (key, key_b, *a1, *b1))

    b2, loan = wait(b, loan)
    b = move(b2[0], ring=1), move(b2[1], ring=-1)
    near = move(after(jnp.concatenate([key, key_b]), b2), group=(1, -1))
    *total, loan_a, loan_b = terms((*own, *lent), a2, (*total, *loan))
    loan = loan_a, loan_b

    a3, loan = wait(a, loan)
    a4 = move(a3[0], ring=1)
    *total, loan_a, loan_b = terms((*own, *lent), b2, (*total, *loan))
    loan = loan_a, loan_b

    b3_left, loan = wait(b[1], loan)
    b4 = move(b3_left, ring=-1)
    total = terms(own, a3, total)
    (b3_right, b3_left), total = wait((b[0], b3_left), total)
    loan = terms(lent, (*a3, b3_right, b3_left), loan)
    a4, loan = wait(a4, loan)
    loan_a, loan_b = terms(lent, (a4,), loan)

    (b4, near), total, loan = lax.optimization_barrier(((b4, near), total, (loan_a, loan_b)))
    last = b3_right, b3_left, a4, b4
    loan_a = terms(lent[:1], (b4,), loan[:1], dtype=RETURN_TYPE)
    back_a = move(loan_a[0], column=1)
    loan_b = terms(lent[1:], (b4,), after(loan[1:], loan_a), dtype=RETURN_TYPE)
    back_b = move(loan_b[0], column=1, core=1)
    own_b = terms(own[1:], (*last, (near, ROWS)), after(total[1:], loan_b))
    other = jnp.concatenate([move(own_b[0][rows], core=1) for rows in THIRDS], axis=0)
    own_a = terms(own[:1], (*last, (near, 0)), after(total[:1], own_b))

    mine = own_a[0] + back_a.astype(jnp.float32)
    other = other + back_b.astype(jnp.float32)
    return jnp.where(first, mine, other), jnp.where(first, other, mine)


def solution(mesh):
    rows = P(("group", "member"), None)
    return jax.shard_map(
        shards, mesh=mesh, in_specs=(rows, rows, P(), P()), out_specs=(rows, rows), check_vma=False
    )
```
